32 devices in a mesh: dfa: 8 (over y, x, core), hid: 4 (over z).
Axes of the slice: x: 2, y: 2, z: 4, core: 2. Of those that a mesh axis runs over, the one named last changes fastest.
Arguments:
- beta_last: bfloat16 [256, 8, 4, 1024], P('dfa', None, 'hid'), may hold values from -6 to 6
- transition: bfloat16 [8, 4, 1024, 32768], P(None, 'hid', None, 'dfa'), may hold values from -0.03125 to 0.03125
- emission: bfloat16 [64, 4, 8192], P(None, 'hid'), may hold values from 0.049804688 to 0.59765625
- successor: int32 [256, 8], replicated, may hold values from 0 to 255
- token_set: int32 [256, 8], replicated, may hold values from 0 to 63
Outputs:
- table: bfloat16 [2, 256, 8, 4, 1024], P(None, 'dfa', None, 'hid')
The draws below stay inside these ranges and needn't reach their ends.
All inputs are finite; a program needn't handle non-finite values.
Results may differ from the reference program's by a relative error of at most 0.0056.
Values may be sent and summed in bfloat16 or wider, within the bound.
A program may use at most 128 MiB of HBM per device.

```python
import math
import jax
import jax.numpy as jnp

Q = 256
H = 32768
NSET = 64
DEG = 8
POS = 2
HC = 1024
HW = 8192
N_DFA = 8
N_HID = 4


def touch_ends(values, key, smallest, high):
    index_at = [jax.random.randint(jax.random.fold_in(key, axis), (), 0, length) for axis, length in enumerate(values.shape)]
    longest = values.shape.index(max(values.shape))
    beside = index_at[:longest] + [(index_at[longest] + 1) % values.shape[longest]] + index_at[longest + 1:]
    return values.at[tuple(index_at)].set(smallest).at[tuple(beside)].set(high)


def block_scale(stream_key, extent, shards, least, largest):
    def one(axis_at, parts):
        heights = jax.random.uniform(jax.random.fold_in(jax.random.fold_in(stream_key, 6), axis_at), (parts,), jnp.float32, least / len(shards), largest / len(shards))
        return jnp.repeat(jnp.exp(heights), extent[axis_at] // parts).reshape((-1,) + (1,) * (len(extent) - axis_at - 1))

    factor_of = one(*shards[0])
    for cut in shards[1:]:
        factor_of = factor_of * one(*cut)
    return factor_of


def bell_draw(own_key, shape, spread, most, pieces=(), kind=jnp.bfloat16):
    result = spread * jax.random.normal(own_key, shape, jnp.float32)
    if pieces:
        result = result * block_scale(own_key, shape, pieces, -0.22, 0.18)
    return jnp.clip(result, -most, most).astype(kind)


def setup_inputs(seed: int = 0) -> dict:
    streams_of = jax.random.split(jax.random.key(seed), 6)
    beta_last = bell_draw(streams_of[0], (Q, N_DFA, N_HID, HC), 1.0, 6.0, ((0, 8), (2, 4)))
    transition = bell_draw(streams_of[1], (N_DFA, N_HID, HC, H), H ** -0.5, 0.03125, ((1, 4), (3, 8)))
    emission = jnp.clip(jnp.exp(math.log(0.59765625) - 2.4849066 * jax.random.uniform(streams_of[2], (NSET, N_HID, HW), jnp.float32) ** block_scale(streams_of[2], (NSET, N_HID, HW), ((1, 4),), -0.2, 0.2)), 0.049804688, 0.59765625).astype(jnp.bfloat16)
    successor = touch_ends(jax.random.randint(streams_of[3], (Q, DEG), 0, Q), jax.random.fold_in(streams_of[3], 1), 0, Q - 1).astype(jnp.int32)
    token_set = touch_ends(jax.random.randint(streams_of[4], (Q, DEG), 0, NSET), jax.random.fold_in(streams_of[4], 1), 0, NSET - 1).astype(jnp.int32)
    return dict(beta_last=beta_last, transition=transition, emission=emission, successor=successor, token_set=token_set)


def reference(beta_last, transition, emission, successor, token_set):
    beta_now = beta_last.reshape(Q, H)
    trans_full = transition.reshape(H, H)
    emission_rows = emission.reshape(NSET, N_HID, N_DFA, HC).transpose(0, 2, 1, 3).reshape(NSET, H)
    results = []
    for position in range(POS):
        total = jnp.zeros((Q, H), jnp.float32)
        for column in range(DEG):
            picked = beta_now[successor[:, column]].astype(jnp.float32)
            weights = emission_rows[token_set[:, column]].astype(jnp.float32)
            total = total + weights * picked
        mixed_rows = total.astype(jnp.bfloat16)
        summed = jnp.dot(mixed_rows, trans_full, preferred_element_type=jnp.float32)
        beta_now = summed.astype(jnp.bfloat16)
        results = [beta_now] + results
    return jnp.stack(results).reshape(POS, Q, N_DFA, N_HID, HC)
```

```python
import jax
import jax.numpy as jnp
from jax import lax
from jax.sharding import PartitionSpec as P

POS = 2


def edge_mix(beta, emission_own, successor, token_set):
    states, nsets = beta.shape[0], emission_own.shape[0]
    total = jnp.zeros(beta.shape, jnp.float32)
    for column in range(successor.shape[1]):
        pick = (successor[:, column][:, None] == jnp.arange(states)[None, :]).astype(jnp.bfloat16)
        kind = (token_set[:, column][:, None] == jnp.arange(nsets)[None, :]).astype(jnp.bfloat16)
        picked = jnp.dot(pick, beta, preferred_element_type=jnp.float32)
        weights = jnp.dot(kind, emission_own, preferred_element_type=jnp.float32)
        total = total + weights * picked
    return total.astype(jnp.bfloat16)


def local(beta_last, transition, emission, successor, token_set):
    owned, blocks, _, cells = beta_last.shape
    width = blocks * cells
    trans_block = transition.reshape(width, transition.shape[3])
    first = lax.axis_index("dfa") * cells
    emission_own = lax.dynamic_slice_in_dim(emission[:, 0, :], first, cells, 1)
    beta = lax.all_to_all(
        beta_last.reshape(owned, width), "dfa", split_axis=1, concat_axis=0, tiled=True
    )
    results = []
    for position in range(POS):
        mixed_own = edge_mix(beta, emission_own, successor, token_set)
        mixed = lax.all_gather(mixed_own, "dfa", axis=1, tiled=True)
        part = jnp.dot(mixed, trans_block, preferred_element_type=jnp.float32)
        beta = lax.psum_scatter(part, "hid", scatter_dimension=1, tiled=True).astype(jnp.bfloat16)
        own_rows = lax.all_to_all(beta, "dfa", split_axis=0, concat_axis=1, tiled=True)
        results = [own_rows.reshape(owned, blocks, 1, cells)] + results
    return jnp.stack(results)


def solution(mesh):
    return jax.shard_map(
        local,
        mesh=mesh,
        in_specs=(
            P("dfa", None, "hid", None),
            P(None, "hid", None, "dfa"),
            P(None, "hid", None),
            P(),
            P(),
        ),
        out_specs=P(None, "dfa", None, "hid", None),
        check_vma=False,
    )
```

```python
import functools

import jax
import jax.numpy as jnp
from jax import lax
from jax.experimental import pallas as pl
from jax.experimental.pallas import tpu as pltpu
from jax.sharding import PartitionSpec as P

POS = 2


def edge_mix(beta, emission_own, successor, token_set):
    states, nsets = beta.shape[0], emission_own.shape[0]
    total = jnp.zeros(beta.shape, jnp.float32)
    for column in range(successor.shape[1]):
        pick = (successor[:, column][:, None] == jnp.arange(states)[None, :]).astype(jnp.bfloat16)
        kind = (token_set[:, column][:, None] == jnp.arange(nsets)[None, :]).astype(jnp.bfloat16)
        picked = jnp.dot(pick, beta, preferred_element_type=jnp.float32)
        weights = jnp.dot(kind, emission_own, preferred_element_type=jnp.float32)
        total = total + weights * picked
    return total.astype(jnp.bfloat16)


PARTS = 2
SLOTS = 6
STEP_COLS = 512
BLOCK_ORDER = (0, 1, 2, 4, 3, 5, 6, 7)


def fused_kernel(
    n_dfa, n_hid,
    beta_in, w_hbm, emis, succ, tok, out,
    mixed, weight, pick, rs_send, rs_recv, acc, own, beta, beta_recv, w_slot,
    a2a_send, a2a_recv, ag_send, ag_recv, sum_send, sum_recv, out_send, out_recv, out_local, w_sem,
):
    d, k = lax.axis_index("dfa"), lax.axis_index("hid")
    core, x, y = lax.rem(d, 2), lax.rem(d // 2, 2), d // 4
    flips = (1 - 2 * core, 2 - 4 * x, 4 - 8 * y)
    owned, cells = beta_in.shape[1], beta_in.shape[2]
    states, degree = succ.shape
    sub = cells // PARTS
    out_cols = w_hbm.shape[2]
    half = states // 2
    sends = []

    def flip(bits):
        place = d
        for bit in range(3):
            if bits >> bit & 1:
                place = place + flips[bit]
        return place

    def remote(source, target, send_sem, recv_sem, where):
        return pltpu.make_async_remote_copy(
            src_ref=source, dst_ref=target, send_sem=send_sem, recv_sem=recv_sem,
            device_id=where, device_id_type=pl.DeviceIdType.MESH,
        )

    def send(*copy):
        sends.append(remote(*copy))
        sends[-1].start()

    order = [(pos, s, i) for pos in range(POS) for s in range(PARTS) for i in range(n_dfa)]

    def w_copy(n):
        _, s, i = order[n]
        return pltpu.make_async_copy(
            w_hbm.at[flip(BLOCK_ORDER[i]), pl.ds(s * sub, sub)], w_slot.at[n % SLOTS], w_sem.at[n % SLOTS]
        )

    for n in range(SLOTS):
        w_copy(n).start()

    barrier = pltpu.get_barrier_semaphore()
    for rel in range(1, n_dfa):
        pl.semaphore_signal(
            barrier, inc=1, device_id={"dfa": lax.rem(d + rel, n_dfa)}, device_id_type=pl.DeviceIdType.MESH
        )
    for rel in range(1, n_hid):
        pl.semaphore_signal(
            barrier, inc=1, device_id={"hid": lax.rem(k + rel, n_hid)}, device_id_type=pl.DeviceIdType.MESH
        )
    for j in range(degree):
        ids = lax.broadcasted_iota(jnp.int32, (states, states), 1)
        pick[j] = jnp.where(succ[:, j:j + 1] == ids, 1.0, 0.0).astype(jnp.bfloat16)
    pl.semaphore_wait(barrier, n_dfa - 1 + n_hid - 1)

    def rows_of(device):
        return pl.ds(pl.multiple_of(device * owned, owned), owned)

    for rel in range(1, n_dfa):
        other = lax.rem(d + rel, n_dfa)
        send(beta_in.at[other], beta_recv.at[rows_of(d)], a2a_send.at[rel - 1], a2a_recv.at[rel - 1], {"dfa": other})
    beta_recv[rows_of(d), :] = beta_in[d]
    for j in range(degree):
        sets = lax.broadcasted_iota(jnp.int32, (states, emis.shape[0]), 1)
        kind = jnp.where(tok[:, j:j + 1] == sets, 1.0, 0.0).astype(jnp.bfloat16)
        weight[j] = jnp.dot(kind, emis[...], preferred_element_type=jnp.float32).astype(jnp.bfloat16)
    for rel in range(1, n_dfa):
        source = lax.rem(d + n_dfa - rel, n_dfa)
        landed = beta_recv.at[rows_of(source)]
        remote(landed, landed, a2a_send.at[rel - 1], a2a_recv.at[rel - 1], {"dfa": source}).wait_recv()

    near, along_x, along_y = {"dfa": flip(1)}, {"dfa": flip(2)}, {"dfa": flip(4)}
    upper, lower = pl.ds(0, half), pl.ds(half, half)

    def gather_send(pos, s, kind, place, where):
        send(place, place, ag_send.at[pos, s, kind], ag_recv.at[pos, s, kind], where)

    def gather_wait(pos, s, kind, place):
        remote(place, place, ag_send.at[pos, s, kind], ag_recv.at[pos, s, kind], near).wait_recv()

    def mix(pos, s, values, first):
        for c in range(0, sub, 256):
            total = jnp.zeros((states, 256), jnp.float32)
            for j in range(degree):
                picked = jnp.dot(pick[j], values[:, first + c:first + c + 256], preferred_element_type=jnp.float32)
                total = total + weight[j, :, s * sub + c:s * sub + c + 256].astype(jnp.float32) * picked
            mixed[pos, s, d, :, c:c + 256] = total.astype(jnp.bfloat16)
        place = mixed.at[pos, s, d]
        gather_send(pos, s, 1, place, along_x)
        gather_send(pos, s, 2, place, along_y)
        gather_send(pos, s, 0, place, near)

    def relay(pos, s):
        from_x, from_y = mixed.at[pos, s, flip(2)], mixed.at[pos, s, flip(4)]
        gather_wait(pos, s, 1, from_x)
        gather_send(pos, s, 3, from_x.at[upper], along_y)
        gather_send(pos, s, 5, from_x, near)
        gather_wait(pos, s, 2, from_y)
        gather_send(pos, s, 4, from_y.at[lower], along_x)
        gather_send(pos, s, 6, from_y, near)

    def multiply(pos, s):
        for i, bits in enumerate(BLOCK_ORDER):
            place = mixed.at[pos, s, flip(bits)]
            if bits == 1:
                gather_wait(pos, s, 0, place)
            if bits == 2:
                relay(pos, s)
            if bits == 3:
                gather_wait(pos, s, 5, place)
            if bits == 5:
                gather_wait(pos, s, 6, place)
            if bits == 6:
                gather_wait(pos, s, 3, place.at[upper])
                gather_send(pos, s, 7, place.at[upper], near)
                gather_wait(pos, s, 4, place.at[lower])
                gather_send(pos, s, 8, place.at[lower], near)
            if bits == 7:
                gather_wait(pos, s, 7, place.at[upper])
                gather_wait(pos, s, 8, place.at[lower])
            n = (pos * PARTS + s) * n_dfa + i
            w_copy(n).wait()
            slot = n % SLOTS

            def product(cols):
                return jnp.dot(place[...], w_slot[slot, :, cols], preferred_element_type=jnp.float32)

            if i < n_dfa - 1 or s < PARTS - 1:

                @pl.loop(0, out_cols // STEP_COLS)
                def _(step):
                    cols = pl.ds(pl.multiple_of(step * STEP_COLS, STEP_COLS), STEP_COLS)
                    if s == 0 and i == 0:
                        acc[:, cols] = product(cols)
                    else:
                        acc[:, cols] += product(cols)

            else:
                for part in range(PARTS):
                    for rel in (2, 1, 3, 0):
                        other = lax.rem(k + rel, n_hid)
                        cols = pl.ds(pl.multiple_of(other * cells + part * sub, sub), sub)
                        total = acc[:, cols] + product(cols)
                        if rel == 0:
                            own[part] = total
                            continue
                        rs_send[pos, part, rel - 1] = total.astype(jnp.bfloat16)
                        send(
                            rs_send.at[pos, part, rel - 1], rs_recv.at[pos, part, rel - 1],
                            sum_send.at[pos, part, rel - 1], sum_recv.at[pos, part, rel - 1], {"hid": other},
                        )
            if n + SLOTS < len(order):
                w_copy(n + SLOTS).start()

    def finish_sum(pos, s):
        total = own[s]
        for rel in range(1, n_hid):
            landed = rs_recv.at[pos, s, rel - 1]
            remote(
                landed, landed, sum_send.at[pos, s, rel - 1], sum_recv.at[pos, s, rel - 1],
                {"hid": lax.rem(k + n_hid - rel, n_hid)},
            ).wait_recv()
            total = total + landed[...].astype(jnp.float32)
        beta[pos, s] = total.astype(jnp.bfloat16)

    def local_out(pos, s):
        return pltpu.make_async_copy(
            beta.at[pos, s, rows_of(d)], out.at[POS - 1 - pos, s, d], out_local.at[pos, s]
        )

    def hand_out(pos, s):
        for rel in range(1, n_dfa):
            other = lax.rem(d + rel, n_dfa)
            send(
                beta.at[pos, s, rows_of(other)], out.at[POS - 1 - pos, s, d],
                out_send.at[pos, s, rel - 1], out_recv.at[pos, s, rel - 1], {"dfa": other},
            )
        local_out(pos, s).start()

    for s in range(PARTS):
        mix(0, s, beta_recv, s * sub)
    for s in range(PARTS):
        multiply(0, s)
    for pos in range(1, POS):
        for s in range(PARTS):
            finish_sum(pos - 1, s)
            mix(pos, s, beta.at[pos - 1, s], 0)
            hand_out(pos - 1, s)
            multiply(pos, s)
    for s in range(PARTS):
        finish_sum(POS - 1, s)
        hand_out(POS - 1, s)
    for pos in range(POS):
        for s in range(PARTS):
            for rel in range(1, n_dfa):
                source = lax.rem(d + n_dfa - rel, n_dfa)
                landed = out.at[POS - 1 - pos, s, source]
                remote(
                    landed, landed, out_send.at[pos, s, rel - 1], out_recv.at[pos, s, rel - 1], {"dfa": source}
                ).wait_recv()
            local_out(pos, s).wait()
    for copy in sends:
        copy.wait_send()


def fused(n_dfa, n_hid, beta_last, transition, emission, successor, token_set):
    owned, blocks, _, cells = beta_last.shape
    states, degree = successor.shape
    sub = cells // PARTS
    out_cols = transition.shape[3]
    first = lax.axis_index("dfa") * cells
    emission_own = lax.dynamic_slice_in_dim(emission[:, 0, :], first, cells, 1)
    beta_in = beta_last[:, :, 0, :].transpose(1, 0, 2)
    w = transition[:, 0]
    bf16, f32, dma = jnp.bfloat16, jnp.float32, pltpu.SemaphoreType.DMA
    vmem, anywhere = pl.BlockSpec(memory_space=pltpu.VMEM), pl.BlockSpec(memory_space=pl.ANY)
    table = pl.pallas_call(
        functools.partial(fused_kernel, n_dfa, n_hid),
        out_shape=jax.ShapeDtypeStruct((POS, PARTS, blocks, owned, sub), bf16),
        in_specs=[vmem, anywhere, vmem, vmem, vmem],
        out_specs=anywhere,
        scratch_shapes=[
            pltpu.VMEM((POS, PARTS, n_dfa, states, sub), bf16),
            pltpu.VMEM((degree, states, cells), bf16),
            pltpu.VMEM((degree, states, states), bf16),
            pltpu.VMEM((POS, PARTS, n_hid - 1, states, sub), bf16),
            pltpu.VMEM((POS, PARTS, n_hid - 1, states, sub), bf16),
            pltpu.VMEM((states, out_cols), f32),
            pltpu.VMEM((PARTS, states, sub), f32),
            pltpu.VMEM((POS, PARTS, states, sub), bf16),
            pltpu.VMEM((states, cells), bf16),
            pltpu.VMEM((SLOTS, sub, out_cols), bf16),
            dma((n_dfa - 1,)),
            dma((n_dfa - 1,)),
            dma((POS, PARTS, 9)),
            dma((POS, PARTS, 9)),
            dma((POS, PARTS, n_hid - 1)),
            dma((POS, PARTS, n_hid - 1)),
            dma((POS, PARTS, n_dfa - 1)),
            dma((POS, PARTS, n_dfa - 1)),
            dma((POS, PARTS)),
            dma((SLOTS,)),
        ],
        compiler_params=pltpu.CompilerParams(
            collective_id=0, has_side_effects=True, vmem_limit_bytes=60 * 2**20
        ),
        cost_estimate=pl.CostEstimate(
            flops=2 * POS * states * blocks * cells * out_cols,
            bytes_accessed=2 * POS * blocks * cells * out_cols,
            transcendentals=0,
        ),
    )(beta_in, w, emission_own, successor, token_set)
    return table.transpose(0, 3, 2, 1, 4).reshape(POS, owned, blocks, 1, cells)


def local(beta_last, transition, emission, successor, token_set):
    owned, blocks, _, cells = beta_last.shape
    width = blocks * cells
    trans_block = transition.reshape(width, transition.shape[3])
    first = lax.axis_index("dfa") * cells
    emission_own = lax.dynamic_slice_in_dim(emission[:, 0, :], first, cells, 1)
    beta = lax.all_to_all(
        beta_last.reshape(owned, width), "dfa", split_axis=1, concat_axis=0, tiled=True
    )
    results = []
    for position in range(POS):
        mixed_own = edge_mix(beta, emission_own, successor, token_set)
        mixed = lax.all_gather(mixed_own, "dfa", axis=1, tiled=True)
        part = jnp.dot(mixed, trans_block, preferred_element_type=jnp.float32)
        beta = lax.psum_scatter(part, "hid", scatter_dimension=1, tiled=True).astype(jnp.bfloat16)
        own_rows = lax.all_to_all(beta, "dfa", split_axis=0, concat_axis=1, tiled=True)
        results = [own_rows.reshape(owned, blocks, 1, cells)] + results
    return jnp.stack(results)


def solution(mesh):
    n_dfa, n_hid = mesh.shape["dfa"], mesh.shape["hid"]

    def body(beta_last, transition, emission, successor, token_set):
        owned, blocks, _, cells = beta_last.shape
        fits = n_dfa == blocks == 8 and n_hid == 4 and cells % (256 * PARTS) == 0 and owned % 16 == 0
        run = functools.partial(fused, n_dfa, n_hid) if fits else local
        return run(beta_last, transition, emission, successor, token_set)

    return jax.shard_map(
        body,
        mesh=mesh,
        in_specs=(
            P("dfa", None, "hid", None),
            P(None, "hid", None, "dfa"),
            P(None, "hid", None),
            P(),
            P(),
        ),
        out_specs=P(None, "dfa", None, "hid", None),
        check_vma=False,
    )
```

```python
import functools

import jax
import jax.numpy as jnp
from jax import lax
from jax.experimental import pallas as pl
from jax.experimental.pallas import tpu as pltpu
from jax.sharding import PartitionSpec as P

POS = 2


def edge_mix(beta, emission_own, successor, token_set):
    states, nsets = beta.shape[0], emission_own.shape[0]
    total = jnp.zeros(beta.shape, jnp.float32)
    for column in range(successor.shape[1]):
        pick = (successor[:, column][:, None] == jnp.arange(states)[None, :]).astype(jnp.bfloat16)
        kind = (token_set[:, column][:, None] == jnp.arange(nsets)[None, :]).astype(jnp.bfloat16)
        picked = jnp.dot(pick, beta, preferred_element_type=jnp.float32)
        weights = jnp.dot(kind, emission_own, preferred_element_type=jnp.float32)
        total = total + weights * picked
    return total.astype(jnp.bfloat16)


PARTS = 2
SLOTS = 6
BLOCK_ORDER = (0, 1, 2, 4, 3, 5, 6, 7)


def fused_kernel(
    n_dfa, n_hid,
    beta_in, w_hbm, emission, succ, tok, out,
    mixed, weight, pick, rs_send, rs_recv, acc, own, beta, beta_recv, emis, w_slot,
    a2a_send, a2a_recv, ag_send, ag_recv, sum_send, sum_recv, out_send, out_recv, out_local, w_sem, emis_sem,
):
    d, k = lax.axis_index("dfa"), lax.axis_index("hid")
    core, x, y = lax.rem(d, 2), lax.rem(d // 2, 2), d // 4
    flips = (1 - 2 * core, 2 - 4 * x, 4 - 8 * y)
    owned, cells = beta_in.shape[1], beta_in.shape[2]
    degree, states = succ.shape
    sub = cells // PARTS
    groups = w_hbm.shape[2] // sub
    last = PARTS - 1
    half = states // 2
    sends = []

    def flip(bits):
        place = d
        for bit in range(3):
            if bits >> bit & 1:
                place = place + flips[bit]
        return place

    def remote(source, target, send_sem, recv_sem, where):
        return pltpu.make_async_remote_copy(
            src_ref=source, dst_ref=target, send_sem=send_sem, recv_sem=recv_sem,
            device_id=where, device_id_type=pl.DeviceIdType.MESH,
        )

    def send(*copy):
        sends.append(remote(*copy))
        sends[-1].start()

    inner, high = lax.rem((k + 1) // 2, 2), k // 2

    def by_role(at_end, at_inner):
        return at_end + inner * (at_inner - at_end)

    far_end = by_role(3 - k, 3 - 3 * high)
    partner = by_role(1 + high, 3 * high)
    hops = (
        (by_role(far_end, 3 - k), by_role(partner, 3 - k), by_role(1, 3)),
        (by_role(2 - high, partner), by_role(2 - high, partner), by_role(2, 0)),
        (by_role(partner, far_end), by_role(partner, far_end), by_role(0, 1)),
    )
    chunks = [(hops[hop][0], part, hop) for part in range(PARTS) for hop in range(n_hid - 1)]
    chunks += [(k, part, n_hid - 1) for part in range(PARTS)]

    def chunk_cols(chunk):
        block, part, _ = chunk
        return pl.ds(pl.multiple_of(block * cells + part * sub, sub), sub)

    order = [(pos, s, i) for pos in range(POS) for s in range(PARTS) for i in range(n_dfa)]

    def w_column_copy(n):
        _, s, i = order[n]
        return pltpu.make_async_copy(
            w_hbm.at[:, pl.ds(s * sub, sub), chunk_cols(chunks[i])], w_slot.at[n % SLOTS], w_sem.at[n % SLOTS, 0]
        )

    def w_row_copy(n, g):
        _, s, i = order[n]
        cols = pl.ds(pl.multiple_of(g * sub, sub), sub)
        return pltpu.make_async_copy(
            w_hbm.at[flip(BLOCK_ORDER[i]), pl.ds(s * sub, sub), cols],
            w_slot.at[n % SLOTS, g], w_sem.at[n % SLOTS, g],
        )

    def w_start(n):
        if order[n][1] == last:
            w_column_copy(n).start()
        else:
            for g in range(groups):
                w_row_copy(n, g).start()

    emis_copy = pltpu.make_async_copy(
        emission.at[:, pl.ds(pl.multiple_of(d * cells, cells), cells)], emis, emis_sem
    )
    emis_copy.start()
    for n in range(SLOTS):
        w_start(n)

    barrier = pltpu.get_barrier_semaphore()
    for rel in range(1, n_dfa):
        pl.semaphore_signal(
            barrier, inc=1, device_id={"dfa": lax.rem(d + rel, n_dfa)}, device_id_type=pl.DeviceIdType.MESH
        )
    for rel in range(1, n_hid):
        pl.semaphore_signal(
            barrier, inc=1, device_id={"hid": lax.rem(k + rel, n_hid)}, device_id_type=pl.DeviceIdType.MESH
        )
    for j in range(degree):
        ids = lax.broadcasted_iota(jnp.int32, (states, states), 0)
        pick[j] = jnp.where(succ[j:j + 1, :] == ids, 1.0, 0.0).T.astype(jnp.bfloat16)
    pl.semaphore_wait(barrier, n_dfa - 1 + n_hid - 1)

    def rows_of(device):
        return pl.ds(pl.multiple_of(device * owned, owned), owned)

    for rel in range(1, n_dfa):
        other = lax.rem(d + rel, n_dfa)
        send(beta_in.at[other], beta_recv.at[rows_of(d)], a2a_send.at[rel - 1], a2a_recv.at[rel - 1], {"dfa": other})
    beta_recv[rows_of(d), :] = beta_in[d]
    emis_copy.wait()
    for j in range(degree):
        sets = lax.broadcasted_iota(jnp.int32, (emis.shape[0], states), 0)
        kind = jnp.where(tok[j:j + 1, :] == sets, 1.0, 0.0).T.astype(jnp.bfloat16)
        weight[j] = jnp.dot(kind, emis[...], preferred_element_type=jnp.float32).astype(jnp.bfloat16)
    for rel in range(1, n_dfa):
        source = lax.rem(d + n_dfa - rel, n_dfa)
        landed = beta_recv.at[rows_of(source)]
        remote(landed, landed, a2a_send.at[rel - 1], a2a_recv.at[rel - 1], {"dfa": source}).wait_recv()

    near, along_x, along_y = {"dfa": flip(1)}, {"dfa": flip(2)}, {"dfa": flip(4)}
    upper, lower = pl.ds(0, half), pl.ds(half, half)

    def gather_send(pos, s, kind, place, where):
        send(place, place, ag_send.at[pos, s, kind], ag_recv.at[pos, s, kind], where)

    def gather_wait(pos, s, kind, place):
        remote(place, place, ag_send.at[pos, s, kind], ag_recv.at[pos, s, kind], near).wait_recv()

    def mix(pos, s, values, first):
        for c in range(0, sub, 256):
            total = jnp.zeros((states, 256), jnp.float32)
            for j in range(degree):
                picked = jnp.dot(pick[j], values[:, first + c:first + c + 256], preferred_element_type=jnp.float32)
                total = total + weight[j, :, s * sub + c:s * sub + c + 256].astype(jnp.float32) * picked
            mixed[pos, s, d, :, c:c + 256] = total.astype(jnp.bfloat16)
        place = mixed.at[pos, s, d]
        gather_send(pos, s, 1, place, along_x)
        gather_send(pos, s, 2, place, along_y)
        gather_send(pos, s, 0, place, near)

    def relay(pos, s):
        from_x, from_y = mixed.at[pos, s, flip(2)], mixed.at[pos, s, flip(4)]
        gather_wait(pos, s, 1, from_x)
        gather_send(pos, s, 3, from_x.at[upper], along_y)
        gather_send(pos, s, 5, from_x, near)
        gather_wait(pos, s, 2, from_y)
        gather_send(pos, s, 4, from_y.at[lower], along_x)
        gather_send(pos, s, 6, from_y, near)

    def arrive(pos, s, bits):
        place = mixed.at[pos, s, flip(bits)]
        if bits == 1:
            gather_wait(pos, s, 0, place)
        if bits == 3:
            gather_wait(pos, s, 5, place)
        if bits == 5:
            gather_wait(pos, s, 6, place)
        if bits == 6:
            gather_wait(pos, s, 3, place.at[upper])
            gather_send(pos, s, 7, place.at[upper], near)
            gather_wait(pos, s, 4, place.at[lower])
            gather_send(pos, s, 8, place.at[lower], near)
        if bits == 7:
            gather_wait(pos, s, 7, place.at[upper])
            gather_wait(pos, s, 8, place.at[lower])

    def multiply_rows(pos, s, relay_next):
        for i, bits in enumerate(BLOCK_ORDER):
            if bits == 2:
                relay(pos, s)
            if bits == 3 and relay_next:
                relay(pos, s + 1)
            arrive(pos, s, bits)
            place = mixed.at[pos, s, flip(bits)]
            n = (pos * PARTS + s) * n_dfa + i
            slot = n % SLOTS

            @pl.loop(0, groups)
            def _(g):
                w_row_copy(n, g).wait()
                cols = pl.ds(pl.multiple_of(g * sub, sub), sub)
                product = jnp.dot(place[...], w_slot[slot, g], preferred_element_type=jnp.float32)
                if s == 0 and i == 0:
                    acc[:, cols] = product
                else:
                    acc[:, cols] += product

            if n + SLOTS < len(order):
                w_start(n + SLOTS)

    def sum_copy(pos, part, hop):
        _, device, slot = hops[hop]
        return (
            rs_send.at[pos, part, hop], rs_recv.at[pos, part, slot],
            sum_send.at[pos, part, hop], sum_recv.at[pos, part, slot], {"hid": device},
        )

    def sum_wait(pos, part, slot):
        landed = rs_recv.at[pos, part, slot]
        remote(landed, landed, sum_send.at[pos, part, 0], sum_recv.at[pos, part, slot], {"hid": partner}).wait_recv()
        return landed

    def multiply_columns(pos, relay_first):
        if relay_first:
            relay(pos, last)
        for bits in BLOCK_ORDER:
            arrive(pos, last, bits)
        for i, chunk in enumerate(chunks):
            _, part, hop = chunk
            n = (pos * PARTS + last) * n_dfa + i
            slot = n % SLOTS
            cols = chunk_cols(chunk)
            w_column_copy(n).wait()

            @pl.loop(0, n_dfa)
            def _(a):
                acc[:, cols] += jnp.dot(mixed[pos, last, a], w_slot[slot, a], preferred_element_type=jnp.float32)

            if n + SLOTS < len(order):
                w_start(n + SLOTS)
            if hop == n_hid - 1:
                own[part] = acc[:, cols]
                continue
            if hop == n_hid - 2:

                @pl.when(inner == 1)
                def _():
                    acc[:, cols] += sum_wait(pos, part, 1)[...].astype(jnp.float32)

            rs_send[pos, part, hop] = acc[:, cols].astype(jnp.bfloat16)
            send(*sum_copy(pos, part, hop))

    def finish_sum(pos, s):
        own[s] += sum_wait(pos, s, 0)[...].astype(jnp.float32)

        @pl.when(inner == 0)
        def _():
            own[s] += sum_wait(pos, s, 1)[...].astype(jnp.float32)

        @pl.when(inner == 1)
        def _():
            for slot in (3, 2):
                own[s] += sum_wait(pos, s, slot)[...].astype(jnp.float32)

        beta[pos, s] = own[s].astype(jnp.bfloat16)

    def out_place(pos, s, block):
        return out.at[POS - 1 - pos, block, :, pl.ds(s * sub, sub)]

    def local_out(pos, s):
        return pltpu.make_async_copy(
            beta.at[pos, s, rows_of(d)], out_place(pos, s, d), out_local.at[pos, s]
        )

    def hand_out(pos, s):
        for rel in range(1, n_dfa):
            other = lax.rem(d + rel, n_dfa)
            send(
                beta.at[pos, s, rows_of(other)], out_place(pos, s, d),
                out_send.at[pos, s, rel - 1], out_recv.at[pos, s, rel - 1], {"dfa": other},
            )
        local_out(pos, s).start()

    for s in range(PARTS):
        mix(0, s, beta_recv, s * sub)
    for s in range(last):
        multiply_rows(0, s, True)
    multiply_columns(0, False)
    for pos in range(1, POS):
        for s in range(PARTS):
            finish_sum(pos - 1, s)
            mix(pos, s, beta.at[pos - 1, s], 0)
            hand_out(pos - 1, s)
            if s < last:
                multiply_rows(pos, s, False)
            else:
                multiply_columns(pos, True)
    for s in range(PARTS):
        finish_sum(POS - 1, s)
        hand_out(POS - 1, s)
    for pos in range(POS):
        for s in range(PARTS):
            for rel in range(1, n_dfa):
                source = lax.rem(d + n_dfa - rel, n_dfa)
                landed = out_place(pos, s, source)
                remote(
                    landed, landed, out_send.at[pos, s, rel - 1], out_recv.at[pos, s, rel - 1], {"dfa": source}
                ).wait_recv()
            local_out(pos, s).wait()
    for copy in sends:
        copy.wait_send()


def fused(n_dfa, n_hid, beta_last, transition, emission, successor, token_set):
    owned, blocks, _, cells = beta_last.shape
    states, degree = successor.shape
    sub = cells // PARTS
    out_cols = transition.shape[3]
    beta_in = beta_last[:, :, 0, :].transpose(1, 0, 2)
    w = transition[:, 0]
    bf16, f32, dma = jnp.bfloat16, jnp.float32, pltpu.SemaphoreType.DMA
    vmem, anywhere = pl.BlockSpec(memory_space=pltpu.VMEM), pl.BlockSpec(memory_space=pl.ANY)
    table = pl.pallas_call(
        functools.partial(fused_kernel, n_dfa, n_hid),
        out_shape=jax.ShapeDtypeStruct((POS, blocks, owned, cells), bf16),
        in_specs=[vmem, anywhere, anywhere, vmem, vmem],
        out_specs=anywhere,
        scratch_shapes=[
            pltpu.VMEM((POS, PARTS, n_dfa, states, sub), bf16),
            pltpu.VMEM((degree, states, cells), bf16),
            pltpu.VMEM((degree, states, states), bf16),
            pltpu.VMEM((POS, PARTS, n_hid - 1, states, sub), bf16),
            pltpu.VMEM((POS, PARTS, n_hid, states, sub), bf16),
            pltpu.VMEM((states, out_cols), f32),
            pltpu.VMEM((PARTS, states, sub), f32),
            pltpu.VMEM((POS, PARTS, states, sub), bf16),
            pltpu.VMEM((states, cells), bf16),
            pltpu.VMEM((emission.shape[0], cells), bf16),
            pltpu.VMEM((SLOTS, n_dfa, sub, sub), bf16),
            dma((n_dfa - 1,)),
            dma((n_dfa - 1,)),
            dma((POS, PARTS, 9)),
            dma((POS, PARTS, 9)),
            dma((POS, PARTS, n_hid - 1)),
            dma((POS, PARTS, n_hid)),
            dma((POS, PARTS, n_dfa - 1)),
            dma((POS, PARTS, n_dfa - 1)),
            dma((POS, PARTS)),
            dma((SLOTS, n_dfa)),
            dma,
        ],
        compiler_params=pltpu.CompilerParams(
            collective_id=0, has_side_effects=True, vmem_limit_bytes=60 * 2**20
        ),
        cost_estimate=pl.CostEstimate(
            flops=2 * POS * states * blocks * cells * out_cols,
            bytes_accessed=2 * POS * blocks * cells * out_cols,
            transcendentals=0,
        ),
    )(beta_in, w, emission[:, 0, :], successor.T, token_set.T)
    return table.transpose(0, 2, 1, 3).reshape(POS, owned, blocks, 1, cells)


def local(beta_last, transition, emission, successor, token_set):
    owned, blocks, _, cells = beta_last.shape
    width = blocks * cells
    trans_block = transition.reshape(width, transition.shape[3])
    first = lax.axis_index("dfa") * cells
    emission_own = lax.dynamic_slice_in_dim(emission[:, 0, :], first, cells, 1)
    beta = lax.all_to_all(
        beta_last.reshape(owned, width), "dfa", split_axis=1, concat_axis=0, tiled=True
    )
    results = []
    for position in range(POS):
        mixed_own = edge_mix(beta, emission_own, successor, token_set)
        mixed = lax.all_gather(mixed_own, "dfa", axis=1, tiled=True)
        part = jnp.dot(mixed, trans_block, preferred_element_type=jnp.float32)
        beta = lax.psum_scatter(part, "hid", scatter_dimension=1, tiled=True).astype(jnp.bfloat16)
        own_rows = lax.all_to_all(beta, "dfa", split_axis=0, concat_axis=1, tiled=True)
        results = [own_rows.reshape(owned, blocks, 1, cells)] + results
    return jnp.stack(results)


def solution(mesh):
    n_dfa, n_hid = mesh.shape["dfa"], mesh.shape["hid"]

    def body(beta_last, transition, emission, successor, token_set):
        owned, blocks, _, cells = beta_last.shape
        fits = n_dfa == blocks == 8 and n_hid == 4 and PARTS == 2 and cells % (256 * PARTS) == 0 and owned % 16 == 0
        fits = fits and transition.shape[3] == n_hid * cells
        run = functools.partial(fused, n_dfa, n_hid) if fits else local
        return run(beta_last, transition, emission, successor, token_set)

    return jax.shard_map(
        body,
        mesh=mesh,
        in_specs=(
            P("dfa", None, "hid", None),
            P(None, "hid", None, "dfa"),
            P(None, "hid", None),
            P(),
            P(),
        ),
        out_specs=P(None, "dfa", None, "hid", None),
        check_vma=False,
    )
```

```python
import functools

import jax
import jax.numpy as jnp
from jax import lax
from jax.experimental import pallas as pl
from jax.experimental.pallas import tpu as pltpu
from jax.sharding import PartitionSpec as P

POS = 2


def edge_mix(beta, emission_own, successor, token_set):
    states, nsets = beta.shape[0], emission_own.shape[0]
    total = jnp.zeros(beta.shape, jnp.float32)
    for column in range(successor.shape[1]):
        pick = (successor[:, column][:, None] == jnp.arange(states)[None, :]).astype(jnp.bfloat16)
        kind = (token_set[:, column][:, None] == jnp.arange(nsets)[None, :]).astype(jnp.bfloat16)
        picked = jnp.dot(pick, beta, preferred_element_type=jnp.float32)
        weights = jnp.dot(kind, emission_own, preferred_element_type=jnp.float32)
        total = total + weights * picked
    return total.astype(jnp.bfloat16)


PARTS = 2
SLOTS = 6
BLOCK_ORDER = (0, 1, 2, 4, 3, 5, 6, 7)


def fused_kernel(
    n_dfa, n_hid,
    beta_in, w_hbm, emission, succ, tok, out,
    mixed, weight, pick, rs_send, rs_recv, acc, own, beta, beta_recv, emis, w_slot,
    a2a_send, a2a_recv, ag_send, ag_recv, sum_send, sum_recv, out_send, out_recv, out_local, w_sem, emis_sem,
):
    d, k = lax.axis_index("dfa"), lax.axis_index("hid")
    core, x, y = lax.rem(d, 2), lax.rem(d // 2, 2), d // 4
    flips = (1 - 2 * core, 2 - 4 * x, 4 - 8 * y)
    owned, cells = beta_in.shape[1], beta_in.shape[2]
    degree, states = succ.shape
    sub = cells // PARTS
    groups = w_hbm.shape[2] // sub
    last = PARTS - 1
    half = states // 2
    sends = []

    def flip(bits):
        place = d
        for bit in range(3):
            if bits >> bit & 1:
                place = place + flips[bit]
        return place

    def remote(source, target, send_sem, recv_sem, where):
        return pltpu.make_async_remote_copy(
            src_ref=source, dst_ref=target, send_sem=send_sem, recv_sem=recv_sem,
            device_id=where, device_id_type=pl.DeviceIdType.MESH,
        )

    def send(*copy):
        sends.append(remote(*copy))
        sends[-1].start()

    inner, high = lax.rem((k + 1) // 2, 2), k // 2

    def by_role(at_end, at_inner):
        return at_end + inner * (at_inner - at_end)

    far_end = by_role(3 - k, 3 - 3 * high)
    partner = by_role(1 + high, 3 * high)
    hops = (
        (by_role(far_end, 3 - k), by_role(partner, 3 - k), by_role(1, 3)),
        (by_role(2 - high, partner), by_role(2 - high, partner), by_role(2, 0)),
        (by_role(partner, far_end), by_role(partner, far_end), by_role(0, 1)),
    )
    chunks = [(hops[hop][0], part, hop) for part in range(PARTS) for hop in range(n_hid - 1)]
    chunks += [(k, part, n_hid - 1) for part in range(PARTS)]

    def chunk_cols(chunk):
        block, part, _ = chunk
        return pl.ds(pl.multiple_of(block * cells + part * sub, sub), sub)

    order = [(pos, s, i) for pos in range(POS) for s in range(PARTS) for i in range(n_dfa)]

    def w_column_copy(n):
        _, s, i = order[n]
        return pltpu.make_async_copy(
            w_hbm.at[:, pl.ds(s * sub, sub), chunk_cols(chunks[i])], w_slot.at[n % SLOTS], w_sem.at[n % SLOTS, 0]
        )

    def w_row_copy(n, g):
        _, s, i = order[n]
        cols = pl.ds(pl.multiple_of(g * sub, sub), sub)
        return pltpu.make_async_copy(
            w_hbm.at[flip(BLOCK_ORDER[i]), pl.ds(s * sub, sub), cols],
            w_slot.at[n % SLOTS, g], w_sem.at[n % SLOTS, g],
        )

    def w_start(n):
        if order[n][1] == last:
            w_column_copy(n).start()
        else:
            for g in range(groups):
                w_row_copy(n, g).start()

    emis_copy = pltpu.make_async_copy(
        emission.at[:, pl.ds(pl.multiple_of(d * cells, cells), cells)], emis, emis_sem
    )
    emis_copy.start()
    for n in range(SLOTS):
        w_start(n)

    barrier = pltpu.get_barrier_semaphore()
    for rel in range(1, n_dfa):
        pl.semaphore_signal(
            barrier, inc=1, device_id={"dfa": lax.rem(d + rel, n_dfa)}, device_id_type=pl.DeviceIdType.MESH
        )
    for rel in range(1, n_hid):
        pl.semaphore_signal(
            barrier, inc=1, device_id={"hid": lax.rem(k + rel, n_hid)}, device_id_type=pl.DeviceIdType.MESH
        )
    for j in range(degree):
        ids = lax.broadcasted_iota(jnp.int32, (states, states), 0)
        pick[j] = jnp.where(succ[j:j + 1, :] == ids, 1.0, 0.0).T.astype(jnp.bfloat16)
    pl.semaphore_wait(barrier, n_dfa - 1 + n_hid - 1)

    def rows_of(device):
        return pl.ds(pl.multiple_of(device * owned, owned), owned)

    for s in range(PARTS):
        cols = pl.ds(s * sub, sub)
        for rel in range(1, n_dfa):
            other = lax.rem(d + rel, n_dfa)
            send(
                beta_in.at[other, :, cols], beta_recv.at[rows_of(d), cols],
                a2a_send.at[s, rel - 1], a2a_recv.at[s, rel - 1], {"dfa": other},
            )
    beta_recv[rows_of(d), :] = beta_in[d]
    emis_copy.wait()
    for j in range(degree):
        sets = lax.broadcasted_iota(jnp.int32, (emis.shape[0], states), 0)
        kind = jnp.where(tok[j:j + 1, :] == sets, 1.0, 0.0).T.astype(jnp.bfloat16)
        weight[j] = jnp.dot(kind, emis[...], preferred_element_type=jnp.float32).astype(jnp.bfloat16)

    def beta_wait(s):
        for rel in range(1, n_dfa):
            source = lax.rem(d + n_dfa - rel, n_dfa)
            landed = beta_recv.at[rows_of(source), pl.ds(s * sub, sub)]
            remote(landed, landed, a2a_send.at[s, rel - 1], a2a_recv.at[s, rel - 1], {"dfa": source}).wait_recv()

    near, along_x, along_y = {"dfa": flip(1)}, {"dfa": flip(2)}, {"dfa": flip(4)}
    upper, lower = pl.ds(0, half), pl.ds(half, half)

    def gather_send(pos, s, kind, place, where):
        send(place, place, ag_send.at[pos, s, kind], ag_recv.at[pos, s, kind], where)

    def gather_wait(pos, s, kind, place):
        remote(place, place, ag_send.at[pos, s, kind], ag_recv.at[pos, s, kind], near).wait_recv()

    def mix(pos, s, values, first):
        for c in range(0, sub, 256):
            total = jnp.zeros((states, 256), jnp.float32)
            for j in range(degree):
                picked = jnp.dot(pick[j], values[:, first + c:first + c + 256], preferred_element_type=jnp.float32)
                total = total + weight[j, :, s * sub + c:s * sub + c + 256].astype(jnp.float32) * picked
            mixed[pos, s, d, :, c:c + 256] = total.astype(jnp.bfloat16)
        place = mixed.at[pos, s, d]
        gather_send(pos, s, 1, place.at[upper], along_x)
        gather_send(pos, s, 2, place.at[lower], along_y)
        gather_send(pos, s, 9, place.at[lower], along_x)
        gather_send(pos, s, 10, place.at[upper], along_y)
        gather_send(pos, s, 0, place, near)

    def relay(pos, s):
        from_x, from_y = mixed.at[pos, s, flip(2)], mixed.at[pos, s, flip(4)]
        gather_wait(pos, s, 1, from_x.at[upper])
        gather_send(pos, s, 3, from_x.at[upper], along_y)
        gather_wait(pos, s, 2, from_y.at[lower])
        gather_send(pos, s, 4, from_y.at[lower], along_x)
        gather_wait(pos, s, 9, from_x.at[lower])
        gather_send(pos, s, 5, from_x, near)
        gather_wait(pos, s, 10, from_y.at[upper])
        gather_send(pos, s, 6, from_y, near)

    def arrive(pos, s, bits):
        place = mixed.at[pos, s, flip(bits)]
        if bits == 1:
            gather_wait(pos, s, 0, place)
        if bits == 3:
            gather_wait(pos, s, 5, place)
        if bits == 5:
            gather_wait(pos, s, 6, place)
        if bits == 6:
            gather_wait(pos, s, 3, place.at[upper])
            gather_send(pos, s, 7, place.at[upper], near)
            gather_wait(pos, s, 4, place.at[lower])
            gather_send(pos, s, 8, place.at[lower], near)
        if bits == 7:
            gather_wait(pos, s, 7, place.at[upper])
            gather_wait(pos, s, 8, place.at[lower])

    def multiply_rows(pos, s, relay_next):
        for i, bits in enumerate(BLOCK_ORDER):
            if bits == 2:
                relay(pos, s)
            if bits == 3 and relay_next:
                relay(pos, s + 1)
            arrive(pos, s, bits)
            place = mixed.at[pos, s, flip(bits)]
            n = (pos * PARTS + s) * n_dfa + i
            slot = n % SLOTS

            @pl.loop(0, groups)
            def _(g):
                w_row_copy(n, g).wait()
                cols = pl.ds(pl.multiple_of(g * sub, sub), sub)
                product = jnp.dot(place[...], w_slot[slot, g], preferred_element_type=jnp.float32)
                if s == 0 and i == 0:
                    acc[:, cols] = product
                else:
                    acc[:, cols] += product

            if n + SLOTS < len(order):
                w_start(n + SLOTS)

    def sum_copy(pos, part, hop):
        _, device, slot = hops[hop]
        return (
            rs_send.at[pos, part, hop], rs_recv.at[pos, part, slot],
            sum_send.at[pos, part, hop], sum_recv.at[pos, part, slot], {"hid": device},
        )

    def sum_wait(pos, part, slot):
        landed = rs_recv.at[pos, part, slot]
        remote(landed, landed, sum_send.at[pos, part, 0], sum_recv.at[pos, part, slot], {"hid": partner}).wait_recv()
        return landed

    def multiply_columns(pos, relay_first):
        if relay_first:
            relay(pos, last)
        for bits in BLOCK_ORDER:
            arrive(pos, last, bits)
        for i, chunk in enumerate(chunks):
            _, part, hop = chunk
            n = (pos * PARTS + last) * n_dfa + i
            slot = n % SLOTS
            cols = chunk_cols(chunk)
            w_column_copy(n).wait()

            @pl.loop(0, n_dfa)
            def _(a):
                acc[:, cols] += jnp.dot(mixed[pos, last, a], w_slot[slot, a], preferred_element_type=jnp.float32)

            if n + SLOTS < len(order):
                w_start(n + SLOTS)
            if hop == n_hid - 1:
                own[part] = acc[:, cols]
                continue
            if hop == n_hid - 2:

                @pl.when(inner == 1)
                def _():
                    acc[:, cols] += sum_wait(pos, part, 1)[...].astype(jnp.float32)

            rs_send[pos, part, hop] = acc[:, cols].astype(jnp.bfloat16)
            send(*sum_copy(pos, part, hop))

    def finish_sum(pos, s):
        own[s] += sum_wait(pos, s, 0)[...].astype(jnp.float32)

        @pl.when(inner == 0)
        def _():
            own[s] += sum_wait(pos, s, 1)[...].astype(jnp.float32)

        @pl.when(inner == 1)
        def _():
            for slot in (3, 2):
                own[s] += sum_wait(pos, s, slot)[...].astype(jnp.float32)

        beta[pos, s] = own[s].astype(jnp.bfloat16)

    def out_place(pos, s, block):
        return out.at[POS - 1 - pos, block, :, pl.ds(s * sub, sub)]

    def local_out(pos, s):
        return pltpu.make_async_copy(
            beta.at[pos, s, rows_of(d)], out_place(pos, s, d), out_local.at[pos, s]
        )

    def hand_out(pos, s):
        for rel in range(1, n_dfa):
            other = lax.rem(d + rel, n_dfa)
            send(
                beta.at[pos, s, rows_of(other)], out_place(pos, s, d),
                out_send.at[pos, s, rel - 1], out_recv.at[pos, s, rel - 1], {"dfa": other},
            )
        local_out(pos, s).start()

    for s in range(PARTS):
        beta_wait(s)
        mix(0, s, beta_recv, s * sub)
    for s in range(last):
        multiply_rows(0, s, True)
    multiply_columns(0, False)
    for pos in range(1, POS):
        for s in range(PARTS):
            finish_sum(pos - 1, s)
            mix(pos, s, beta.at[pos - 1, s], 0)
            if s < last:
                multiply_rows(pos, s, False)
            else:
                multiply_columns(pos, True)
        for s in range(PARTS):
            hand_out(pos - 1, s)
    for s in range(PARTS):
        finish_sum(POS - 1, s)
        hand_out(POS - 1, s)
    for pos in range(POS):
        for s in range(PARTS):
            for rel in range(1, n_dfa):
                source = lax.rem(d + n_dfa - rel, n_dfa)
                landed = out_place(pos, s, source)
                remote(
                    landed, landed, out_send.at[pos, s, rel - 1], out_recv.at[pos, s, rel - 1], {"dfa": source}
                ).wait_recv()
            local_out(pos, s).wait()
    for copy in sends:
        copy.wait_send()


def fused(n_dfa, n_hid, beta_last, transition, emission, successor, token_set):
    owned, blocks, _, cells = beta_last.shape
    states, degree = successor.shape
    sub = cells // PARTS
    out_cols = transition.shape[3]
    beta_in = beta_last[:, :, 0, :].transpose(1, 0, 2)
    w = transition[:, 0]
    bf16, f32, dma = jnp.bfloat16, jnp.float32, pltpu.SemaphoreType.DMA
    vmem, anywhere = pl.BlockSpec(memory_space=pltpu.VMEM), pl.BlockSpec(memory_space=pl.ANY)
    table = pl.pallas_call(
        functools.partial(fused_kernel, n_dfa, n_hid),
        out_shape=jax.ShapeDtypeStruct((POS, blocks, owned, cells), bf16),
        in_specs=[vmem, anywhere, anywhere, vmem, vmem],
        out_specs=anywhere,
        scratch_shapes=[
            pltpu.VMEM((POS, PARTS, n_dfa, states, sub), bf16),
            pltpu.VMEM((degree, states, cells), bf16),
            pltpu.VMEM((degree, states, states), bf16),
            pltpu.VMEM((POS, PARTS, n_hid - 1, states, sub), bf16),
            pltpu.VMEM((POS, PARTS, n_hid, states, sub), bf16),
            pltpu.VMEM((states, out_cols), f32),
            pltpu.VMEM((PARTS, states, sub), f32),
            pltpu.VMEM((POS, PARTS, states, sub), bf16),
            pltpu.VMEM((states, cells), bf16),
            pltpu.VMEM((emission.shape[0], cells), bf16),
            pltpu.VMEM((SLOTS, n_dfa, sub, sub), bf16),
            dma((PARTS, n_dfa - 1)),
            dma((PARTS, n_dfa - 1)),
            dma((POS, PARTS, 11)),
            dma((POS, PARTS, 11)),
            dma((POS, PARTS, n_hid - 1)),
            dma((POS, PARTS, n_hid)),
            dma((POS, PARTS, n_dfa - 1)),
            dma((POS, PARTS, n_dfa - 1)),
            dma((POS, PARTS)),
            dma((SLOTS, n_dfa)),
            dma,
        ],
        compiler_params=pltpu.CompilerParams(
            collective_id=0, has_side_effects=True, vmem_limit_bytes=60 * 2**20
        ),
        cost_estimate=pl.CostEstimate(
            flops=2 * POS * states * blocks * cells * out_cols,
            bytes_accessed=2 * POS * blocks * cells * out_cols,
            transcendentals=0,
        ),
    )(beta_in, w, emission[:, 0, :], successor.T, token_set.T)
    return table.transpose(0, 2, 1, 3).reshape(POS, owned, blocks, 1, cells)


def local(beta_last, transition, emission, successor, token_set):
    owned, blocks, _, cells = beta_last.shape
    width = blocks * cells
    trans_block = transition.reshape(width, transition.shape[3])
    first = lax.axis_index("dfa") * cells
    emission_own = lax.dynamic_slice_in_dim(emission[:, 0, :], first, cells, 1)
    beta = lax.all_to_all(
        beta_last.reshape(owned, width), "dfa", split_axis=1, concat_axis=0, tiled=True
    )
    results = []
    for position in range(POS):
        mixed_own = edge_mix(beta, emission_own, successor, token_set)
        mixed = lax.all_gather(mixed_own, "dfa", axis=1, tiled=True)
        part = jnp.dot(mixed, trans_block, preferred_element_type=jnp.float32)
        beta = lax.psum_scatter(part, "hid", scatter_dimension=1, tiled=True).astype(jnp.bfloat16)
        own_rows = lax.all_to_all(beta, "dfa", split_axis=0, concat_axis=1, tiled=True)
        results = [own_rows.reshape(owned, blocks, 1, cells)] + results
    return jnp.stack(results)


def solution(mesh):
    n_dfa, n_hid = mesh.shape["dfa"], mesh.shape["hid"]

    def body(beta_last, transition, emission, successor, token_set):
        owned, blocks, _, cells = beta_last.shape
        fits = n_dfa == blocks == 8 and n_hid == 4 and PARTS == 2 and cells % (256 * PARTS) == 0 and owned % 16 == 0
        fits = fits and transition.shape[3] == n_hid * cells
        run = functools.partial(fused, n_dfa, n_hid) if fits else local
        return run(beta_last, transition, emission, successor, token_set)

    return jax.shard_map(
        body,
        mesh=mesh,
        in_specs=(
            P("dfa", None, "hid", None),
            P(None, "hid", None, "dfa"),
            P(None, "hid", None),
            P(),
            P(),
        ),
        out_specs=P(None, "dfa", None, "hid", None),
        check_vma=False,
    )
```
